1024 devices in a mesh: row: 128 (over y, z), task: 8 (over x, core).
Axes of the slice: x: 4, y: 8, z: 16, core: 2. Of those that a mesh axis runs over, the one named last changes fastest.
Arguments:
- a_vals: float32 [8192, 8, 4096], P('row', 'task'), may hold values from -0.75 to 0.75
- a_cols: int32 [8192, 8], P('row', 'task'), may hold values from 0 to 8191, as said below
- a_len: int32 [8192], P('row'), may hold values from 1 to 8, as said below
- p_vals: float32 [8192, 2, 4096], P('row'), may hold values from -0.75 to 0.75
- p_cols: int32 [8192, 2], P('row'), may hold values from 0 to 1023, as said below
Outputs:
- c_tiles: float32 [1024, 7, 4096], P(('row', 'task'))
The draws below stay inside these ranges and needn't reach their ends.
Inputs may be any that keep to these rules, and one draw needn't show every extreme that they name: `a_cols`: slot 0 of fine block-row i holds i itself; the 8 columns of a row are distinct and lie in a window of 13 block-rows, i - 6 to i + 6, moved inside 0 to 8191 at the two ends. The live slots of a row are its first a_len ones; the first fine block-row of every slab of 64 has all 8 live and the last has one. `p_cols`: the two entries of fine block-row i are distinct, each one of i // 8 - 1, i // 8, i // 8 + 1.
All inputs are finite; a program needn't handle non-finite values.
Results may differ from the reference program's by a relative error of at most 0.0003.
Values sent between devices are 32-bit elements; how exact they have to be, the bound alone decides.
A program may use at most 128 MiB of HBM per device.

```python
import jax
import jax.numpy as jnp
from jax import lax

TILE = 64
RATIO = 8
FW = 6
KA = 8
PTILES = 2
FR = 64
NF = 8192
NC = 1024


def draw_a_cols(key, part):
    key = jax.random.fold_in(key, 11)
    window = 2 * FW + 1
    row_ids = jnp.arange(NF, dtype=jnp.int32)
    lowest = jnp.clip(row_ids - FW, 0, NF - window)
    places = jnp.arange(window, dtype=jnp.int32)
    scores = jax.random.randint(key, (NF, window), 0, 1 << 20) * window + places[None, :]
    scores = jnp.where(lowest[:, None] + places[None, :] == row_ids[:, None], -1, scores)
    chosen = jnp.argsort(scores, axis=1, stable=True)[:, :KA].astype(jnp.int32)
    return (lowest[:, None] + chosen).astype(jnp.int32)


def draw_a_len(key, part):
    key = jax.random.fold_in(key, 12)
    key_heavy, key_short, key_long = jax.random.split(key, 3)
    heavy_row = jax.random.randint(key_heavy, (NF,), 0, 4) == 0
    short_len = jax.random.randint(key_short, (NF,), 1, KA // 2)
    long_len = jax.random.randint(key_long, (NF,), KA // 2, KA + 1)
    lengths = jnp.where(heavy_row, long_len, short_len)
    position = jnp.arange(NF, dtype=jnp.int32) % FR
    lengths = jnp.where(position == 0, KA, lengths)
    lengths = jnp.where(position == FR - 1, 1, lengths)
    return lengths.astype(jnp.int32)


def draw_p_cols(key, part):
    key = jax.random.fold_in(key, 13)
    home_rows = jnp.arange(NF, dtype=jnp.int32) // RATIO
    dropped = jax.random.randint(key, (NF,), 0, 3)
    dropped = jnp.where(home_rows == 0, 0, dropped)
    dropped = jnp.where(home_rows == NC - 1, 2, dropped)
    first_kept = jnp.where(dropped == 0, 1, 0)
    second_kept = jnp.where(dropped == 2, 1, 2)
    return jnp.stack([home_rows - 1 + first_kept, home_rows - 1 + second_kept], axis=1).astype(jnp.int32)


def block_scale(stream_key, shape, cuts, low, top_value):
    def one(axis_at, shards_of):
        draws = jax.random.uniform(jax.random.fold_in(jax.random.fold_in(stream_key, 6), axis_at), (shards_of,), jnp.float32, low / len(cuts), top_value / len(cuts))
        return jnp.repeat(jnp.exp(draws), shape[axis_at] // shards_of).reshape((-1,) + (1,) * (len(shape) - axis_at - 1))

    level = one(*cuts[0])
    for cut in cuts[1:]:
        level = level * one(*cut)
    return level


def bell_draw(stream_key, shape, scale, most, cuts=(), kind=jnp.bfloat16):
    array = scale * jax.random.normal(stream_key, shape, jnp.float32)
    if cuts:
        array = array * block_scale(stream_key, shape, cuts, -0.22, 0.18)
    return jnp.clip(array, -most, most).astype(kind)


def setup_inputs(seed: int = 0) -> dict:
    key_of = jax.random.split(jax.random.key(seed), 6)
    a_vals = bell_draw(key_of[0], (NF, KA, TILE * TILE), TILE ** -0.5, 0.75, ((0, 128), (1, 8)), jnp.float32)
    a_cols = draw_a_cols(jax.random.fold_in(key_of[5], 71), 0)
    a_len = draw_a_len(jax.random.fold_in(key_of[5], 71), 0)
    p_vals = bell_draw(key_of[3], (NF, PTILES, TILE * TILE), TILE ** -0.5, 0.75, ((0, 128),), jnp.float32)
    p_cols = draw_p_cols(jax.random.fold_in(key_of[5], 71), 0)
    return {"a_vals": a_vals, "a_cols": a_cols, "a_len": a_len, "p_vals": p_vals, "p_cols": p_cols}


highest = lax.Precision.HIGHEST


def band_of(p_vals, p_cols, home_rows):
    offsets = p_cols - home_rows[:, None] + 1
    pieces = []
    for position in range(3):
        chosen = jnp.where((offsets == position)[:, :, None], p_vals, 0.0)
        pieces.append(jnp.sum(chosen, axis=1))
    return jnp.stack(pieces, axis=1)


def place_products(product, shift_ids):
    leading = product.ndim - 3
    placed = 0.0
    for offset in range(3):
        widths = [(0, 0)] * leading + [(offset, 2 - offset), (0, 0), (0, 0)]
        widened = jnp.pad(product, widths)
        placed = placed + jnp.where((shift_ids == offset)[..., None, None, None], widened, 0.0)
    return placed


def coarse_part(own_band, fine_ap, coarse_rows):
    tile_size = fine_ap.shape[-1]
    left_tiles = own_band.reshape(coarse_rows, RATIO, 3, tile_size, tile_size)
    right_tiles = fine_ap.reshape(coarse_rows, RATIO, 5, tile_size, tile_size)
    summed = jnp.einsum('hrdba,hrebc->hdeac', left_tiles, right_tiles, precision=highest)
    partial_value = 0.0
    for offset in range(3):
        partial_value = partial_value + jnp.pad(summed[:, offset], ((offset, 2 - offset), (2 - offset, offset), (0, 0), (0, 0)))
    return partial_value.reshape(coarse_rows + 2, 7, tile_size * tile_size)


def reference(a_vals, a_cols, a_len, p_vals, p_cols):
    fine_total = a_vals.shape[0]
    tile_size = TILE
    groups = fine_total // FR
    ext_ids = jnp.arange(-FW, fine_total + FW, dtype=jnp.int32)
    p_ext = jnp.pad(p_vals, ((FW, FW), (0, 0), (0, 0)))
    cols_ext = jnp.pad(p_cols, ((FW, FW), (0, 0)), constant_values=-8)
    band_ext = band_of(p_ext, cols_ext, ext_ids // RATIO)

    def one_group(group_id):
        first_row = group_id * FR
        a_group = lax.dynamic_slice_in_dim(a_vals, first_row, FR, 0).reshape(FR, KA, tile_size, tile_size)
        columns = lax.dynamic_slice_in_dim(a_cols, first_row, FR, 0)
        lengths = lax.dynamic_slice_in_dim(a_len, first_row, FR, 0)
        local_band = lax.dynamic_slice_in_dim(band_ext, first_row, FR + 2 * FW, 0)
        live_slots = jnp.arange(KA, dtype=jnp.int32)[None, :] < lengths[:, None]
        masked = jnp.where(live_slots[:, :, None, None], a_group, 0.0)
        right_tiles = local_band[columns - first_row + FW].reshape(FR, KA, 3, tile_size, tile_size)
        product = jnp.einsum('ikab,ikdbc->ikdac', masked, right_tiles, precision=highest)
        group_rows = first_row + jnp.arange(FR, dtype=jnp.int32)
        shift_ids = columns // RATIO - (group_rows // RATIO)[:, None] + 1
        fine_ap = jnp.sum(place_products(product, shift_ids), axis=1)
        return coarse_part(local_band[FW:FW + FR], fine_ap, FR // RATIO)

    partials = lax.map(one_group, jnp.arange(groups, dtype=jnp.int32))
    coarse_rows = FR // RATIO
    interior = partials[:, 1:coarse_rows + 1]
    interior = interior.at[1:, 0].add(partials[:-1, coarse_rows + 1])
    interior = interior.at[:-1, coarse_rows - 1].add(partials[1:, 0])
    return interior.reshape(groups * coarse_rows, 7, tile_size * tile_size)
```

```python
import functools

import jax
import jax.numpy as jnp
from jax import lax
from jax.experimental import pallas as pl
from jax.experimental.pallas import tpu as pltpu
from jax.sharding import PartitionSpec as P

TILE = 64
RATIO = 8
FW = 6
SLAB = 64
HALF = 32
MESH = pl.DeviceIdType.MESH
F32 = jnp.float32
BF16 = jnp.bfloat16


def split(x):
    high = x.astype(BF16)
    low = (x - high.astype(F32)).astype(BF16)
    return high, low


def kernel(
    row_count,
    a_hbm,
    acol_any,
    p_hbm,
    pcol_any,
    acol,
    alen,
    pcol,
    out_ref,
    a_own,
    a_sib,
    p_raw,
    p_halo,
    acol_sib_v,
    pcol_halo_v,
    acol_sib,
    pcol_halo,
    band_high,
    band_low,
    left,
    ap_high,
    ap_low,
    sums,
    flat,
    sib_out,
    sib_in,
    edge_out,
    edge_in,
    gathered,
    a_local_sem,
    a_send_sem,
    a_recv_sem,
    p_local_sem,
    halo_send_sem,
    halo_recv_sem,
    int_send_sem,
    int_recv_sem,
    int_local_sem,
    cross_send_sem,
    cross_recv_sem,
    sum_send_sem,
    sum_recv_sem,
):
    row = lax.axis_index("row")
    task = lax.axis_index("task")
    core = task % 2
    chip = task // 2
    other = task + 1 - 2 * core
    beside = (row + row_count + 2 * core - 1) % row_count
    sib_id = (row, other)
    edge_id = (beside, other)

    barrier = pltpu.get_barrier_semaphore()
    for step in range(1, 8):
        pl.semaphore_signal(barrier, inc=1, device_id=(row, (task + step) % 8), device_id_type=MESH)
    pl.semaphore_signal(barrier, inc=1, device_id=edge_id, device_id_type=MESH)

    def home_of(u, which):
        return 3 - u + which * (1 + 2 * u)

    p_copies = []
    for u in (-1, 0, 1, 2, 3):
        first = 32 - 6 * core if u < 0 else 8 * home_of(u, core)
        size = 6 if u < 0 else 8
        copy = pltpu.make_async_copy(
            p_hbm.at[pl.ds(first, size)], p_raw.at[pl.ds(first - 26 * core, size)], p_local_sem.at[u + 1]
        )
        copy.start()
        p_copies.append(copy)
    a_copies = []
    for u in range(4):
        copy = pltpu.make_async_copy(
            a_hbm.at[pl.ds(8 * home_of(u, core), 8)], a_own.at[pl.ds(8 * u, 8)], a_local_sem.at[u]
        )
        copy.start()
        a_copies.append(copy)

    pl.semaphore_wait(barrier, 8)

    acol_copy = pltpu.make_async_remote_copy(
        acol_any, acol_sib_v, int_send_sem.at[0], int_recv_sem.at[0], device_id=sib_id, device_id_type=MESH
    )
    acol_copy.start()
    pcol_copy = pltpu.make_async_remote_copy(
        pcol_any, pcol_halo_v, int_send_sem.at[1], int_recv_sem.at[1], device_id=edge_id, device_id_type=MESH
    )
    pcol_copy.start()
    halo_copy = pltpu.make_async_remote_copy(
        p_hbm.at[pl.ds(58 * core, FW)], p_halo, halo_send_sem, halo_recv_sem, device_id=edge_id, device_id_type=MESH
    )
    halo_copy.start()
    a_sends = []
    for u in range(4):
        copy = pltpu.make_async_remote_copy(
            a_hbm.at[pl.ds(8 * home_of(u, 1 - core), 8)],
            a_sib.at[pl.ds(8 * u, 8)],
            a_send_sem.at[u],
            a_recv_sem.at[u],
            device_id=sib_id,
            device_id_type=MESH,
        )
        copy.start()
        a_sends.append(copy)

    lane = lax.broadcasted_iota(jnp.int32, (HALF, 128), 1)
    lower = lane < TILE
    upper_bit = lane // TILE
    parity_order = upper_bit * TILE + 2 * (lane % HALF) + (lane % TILE) // HALF

    def put_band(tiles, index, offset0, offset1, u_parity):
        x0 = tiles[0]
        x1 = tiles[1]
        r0 = pltpu.roll(x0, TILE, 1)
        r1 = pltpu.roll(x1, TILE, 1)
        even0, odd0 = jnp.where(lower, x0, r0), jnp.where(lower, r0, x0)
        even1, odd1 = jnp.where(lower, x1, r1), jnp.where(lower, r1, x1)
        place0 = offset0 + 1 - u_parity
        place1 = offset1 + 1 - u_parity
        for pair in range(2):
            here = upper_bit + 2 * pair
            take0 = here == place0
            take1 = here == place1
            for part, y0, y1 in ((0, even0, even1), (1, odd0, odd1)):
                high, low = split(jnp.where(take0, y0, jnp.where(take1, y1, 0.0)))
                band_high[index, pl.ds(HALF * part, HALF), pl.ds(128 * pair, 128)] = high
                band_low[index, pl.ds(HALF * part, HALF), pl.ds(128 * pair, 128)] = low

    def offset_of(column, home):
        offset = column - home + 1
        return 2 - offset + core * (2 * offset - 2)

    def prepare(u):
        count = 8 if 0 <= u < 4 else FW
        parity = u % 2

        def one(k, carry):
            if u == 4:
                v = 37 - k + core * (2 * k - 5)
                home = 8 * row - 1 + 9 * core
                at = k + 58 * (1 - core)
                tiles = [p_halo[k, pl.ds(which, HALF, stride=2), :] for which in range(2)]
                offsets = [offset_of(pcol_halo[which, at], home) for which in range(2)]
            else:
                j = (32 - 6 * core if u < 0 else 8 * home_of(u, core)) + k
                v = 31 - j + core * (2 * j - 63)
                home = 8 * row + (4 - core if u < 0 else home_of(u, core))
                tiles = [p_raw[j - 26 * core, pl.ds(which, HALF, stride=2), :] for which in range(2)]
                offsets = [offset_of(pcol[which, j], home) for which in range(2)]
            put_band(tiles, v + FW, offsets[0], offsets[1], parity)
            if 0 <= u < 4:
                for d in range(3):
                    zero = jnp.zeros_like(lane)
                    picked = jnp.where(
                        zero + offsets[0] == d, tiles[0], jnp.where(zero + offsets[1] == d, tiles[1], 0.0)
                    )
                    left[u, d, k // 4, pl.ds(HALF * (k % 4), HALF), :] = picked
            return carry

        lax.fori_loop(0, count, one, 0, unroll=2)

    def products(u):
        home = home_of(u, core)

        def one(k, carry):
            j = 8 * home + k
            length = alen[j]
            zero = jnp.zeros((TILE, 128), jnp.int32)
            total = [0.0, 0.0, 0.0]
            for tiles, columns, slot in ((a_own, acol, task), (a_sib, acol_sib, other)):
                column = columns[0, j] - SLAB * row
                v = jnp.clip(31 - column + core * (2 * column - 63), -FW, HALF + FW - 1)
                live = jnp.where(slot < length, 1.0, 0.0).astype(F32)
                raw = tiles[8 * u + k] * live
                near = jnp.take_along_axis(raw, parity_order, axis=1)
                far = pltpu.roll(near, TILE, 1)
                twice = jnp.concatenate([jnp.where(lower, near, far), jnp.where(lower, far, near)], axis=0)
                high, low = split(twice)
                tile = jnp.concatenate([high, low[:, :TILE]], axis=1)
                right_high = band_high[v + FW]
                right_low = band_low[v + FW]
                right = jnp.concatenate([right_high, right_low, right_high], axis=0)
                product = jnp.dot(tile, right, preferred_element_type=F32)
                first, second = product[:, :128], product[:, 128:]
                shift = ((v + 8) // 8 - 2 + 4) // 2 - (u - 2 + 4) // 2
                still = zero + shift == 0
                total[0] = total[0] + jnp.where(still, first, 0.0)
                total[1] = total[1] + jnp.where(still, second, first)
                total[2] = total[2] + jnp.where(still, 0.0, second)
            at = 256 * (k // 4) + HALF * (k % 4)
            for pair in range(3):
                high, low = split(total[pair])
                for part in range(2):
                    place = pl.ds(pl.multiple_of(at + 128 * part, HALF), HALF)
                    lanes = pl.ds(128 * pair, 128)
                    ap_high[place, lanes] = high[HALF * part : HALF * (part + 1)]
                    ap_low[place, lanes] = low[HALF * part : HALF * (part + 1)]
            return carry

        lax.fori_loop(0, 8, one, 0, unroll=2)

    def coarse(u):
        high_parts, low_parts = [], []
        for d in range(3):
            high_row, low_row = [], []
            for group in range(2):
                high, low = split(left[u, d, group].T)
                high_row += [high[:TILE], high[TILE:]]
                low_row += [low[:TILE], low[TILE:]]
            high_parts.append(jnp.concatenate(high_row, axis=1))
            low_parts.append(jnp.concatenate(low_row, axis=1))
        high = jnp.concatenate(high_parts, axis=0)
        low = jnp.concatenate(low_parts, axis=0)
        result = jnp.dot(high, ap_high[...], preferred_element_type=F32)
        result = result + jnp.dot(high, ap_low[...], preferred_element_type=F32)
        result = result + jnp.dot(low, ap_high[...], preferred_element_type=F32)
        for d in range(3):
            begin = (1, 1 - u % 2, 0)[d]
            fresh = d == 2 or u == 0
            for pair in range(4):
                inside = begin <= pair < begin + 3
                if inside:
                    value = result[TILE * d : TILE * (d + 1), 128 * (pair - begin) : 128 * (pair - begin + 1)]
                    if fresh:
                        sums[u + d, pair] = value
                    else:
                        sums[u + d, pair] += value
                elif fresh:
                    sums[u + d, pair] = jnp.zeros((TILE, 128), F32)

    def flatten(w, deltas, target, correction):
        for delta in deltas:
            place = w + delta
            pair = place // 2 - (w - 3) // 2
            even = sums[w + 1, pair, pl.ds(0, HALF, stride=2), :]
            odd = sums[w + 1, pair, pl.ds(1, HALF, stride=2), :]
            if place % 2 == 0:
                value = jnp.where(lower, even, pltpu.roll(odd, TILE, 1))
            else:
                value = jnp.where(lower, pltpu.roll(even, TILE, 1), odd)
            target[3 + (2 * core - 1) * delta - correction] = value

    mine = core == chip // 2

    def sum_copy(w):
        owner = home_of(w, core)
        copy = pltpu.make_async_remote_copy(
            flat.at[w],
            gathered.at[chip],
            sum_send_sem.at[w],
            sum_recv_sem.at[chip],
            device_id=(row, owner),
            device_id_type=MESH,
        )
        return copy, owner == task

    def send_sum(w):
        copy, local = sum_copy(w)

        @pl.when(local)
        def _():
            gathered[chip] = flat[w]

        @pl.when(jnp.logical_not(local))
        def _():
            copy.start()

    sib_copy = pltpu.make_async_remote_copy(
        sib_out, sib_in, cross_send_sem.at[0], cross_recv_sem.at[0], device_id=sib_id, device_id_type=MESH
    )
    edge_copy = pltpu.make_async_remote_copy(
        edge_out, edge_in, cross_send_sem.at[1], cross_recv_sem.at[1], device_id=edge_id, device_id_type=MESH
    )
    everything = range(-3, 4)

    p_copies[0].wait()
    prepare(-1)
    p_copies[1].wait()
    prepare(0)
    p_copies[2].wait()
    prepare(1)
    acol_copy.wait()
    to_smem = pltpu.make_async_copy(acol_sib_v, acol_sib, int_local_sem.at[0])
    to_smem.start()
    to_smem.wait()
    for u in range(4):
        a_copies[u].wait()
        a_sends[u].wait()
        products(u)
        coarse(u)
        if u == 0:
            flatten(-1, range(-1, 4), sib_out, 2 * core)
            sib_copy.start()
            p_copies[3].wait()
            prepare(2)
        elif u == 1:
            flatten(0, everything, flat.at[0], 0)
            sib_copy.wait()
            begin = 2 - 2 * core
            for k in range(5):
                flat[0, begin + k] += sib_in[k]
            send_sum(0)
            p_copies[4].wait()
            prepare(3)
        elif u == 2:
            flatten(1, everything, flat.at[1], 0)
            send_sum(1)
            halo_copy.wait()
            pcol_copy.wait()
            to_smem = pltpu.make_async_copy(pcol_halo_v, pcol_halo, int_local_sem.at[1])
            to_smem.start()
            to_smem.wait()
            prepare(4)
        else:
            flatten(4, range(-3, 2), edge_out, 2 - 2 * core)
            edge_copy.start()
            flatten(2, everything, flat.at[2], 0)
            send_sum(2)
            flatten(3, everything, flat.at[3], 0)
            edge_copy.wait()
            begin = 2 * core
            for k in range(5):
                flat[3, begin + k] += edge_in[k]
            send_sum(3)

    for w in range(4):
        copy, local = sum_copy(w)

        @pl.when(jnp.logical_not(local))
        def _():
            copy.wait_send()

    for source in range(4):
        copy = pltpu.make_async_remote_copy(
            flat.at[0],
            gathered.at[source],
            sum_send_sem.at[0],
            sum_recv_sem.at[source],
            device_id=(row, other),
            device_id_type=MESH,
        )

        @pl.when(jnp.logical_not(jnp.logical_and(mine, chip == source)))
        def _():
            copy.wait_recv()

    out_ref[...] = (gathered[0] + gathered[1]) + (gathered[2] + gathered[3])


def on_device(row_count, a_vals, a_cols, a_len, p_vals, p_cols):
    a_tiles = a_vals.reshape(SLAB, HALF, 128)
    p_tiles = p_vals.reshape(SLAB, 2, HALF, 128).transpose(0, 2, 1, 3).reshape(SLAB, TILE, 128)
    acol = a_cols.reshape(1, SLAB)
    pcol = p_cols.T
    alen = a_len
    dma = pltpu.SemaphoreType.DMA
    smem = pl.BlockSpec(memory_space=pltpu.SMEM)
    anywhere = pl.BlockSpec(memory_space=pl.ANY)
    out = pl.pallas_call(
        functools.partial(kernel, row_count),
        out_shape=jax.ShapeDtypeStruct((7, HALF, 128), F32),
        in_specs=[anywhere, anywhere, anywhere, anywhere, smem, smem, smem],
        out_specs=pl.BlockSpec(memory_space=pltpu.VMEM),
        scratch_shapes=[
            pltpu.VMEM((HALF, HALF, 128), F32),
            pltpu.VMEM((HALF, HALF, 128), F32),
            pltpu.VMEM((38, TILE, 128), F32),
            pltpu.VMEM((FW, TILE, 128), F32),
            pltpu.VMEM((1, SLAB), jnp.int32),
            pltpu.VMEM((2, SLAB), jnp.int32),
            pltpu.SMEM((1, SLAB), jnp.int32),
            pltpu.SMEM((2, SLAB), jnp.int32),
            pltpu.VMEM((44, TILE, 256), BF16),
            pltpu.VMEM((44, TILE, 256), BF16),
            pltpu.VMEM((4, 3, 2, 128, 128), F32),
            pltpu.VMEM((512, 384), BF16),
            pltpu.VMEM((512, 384), BF16),
            pltpu.VMEM((6, 4, TILE, 128), F32),
            pltpu.VMEM((4, 7, HALF, 128), F32),
            pltpu.VMEM((5, HALF, 128), F32),
            pltpu.VMEM((5, HALF, 128), F32),
            pltpu.VMEM((5, HALF, 128), F32),
            pltpu.VMEM((5, HALF, 128), F32),
            pltpu.VMEM((4, 7, HALF, 128), F32),
            dma((4,)),
            dma((4,)),
            dma((4,)),
            dma((5,)),
            dma,
            dma,
            dma((2,)),
            dma((2,)),
            dma((2,)),
            dma((2,)),
            dma((2,)),
            dma((4,)),
            dma((4,)),
        ],
        compiler_params=pltpu.CompilerParams(
            collective_id=0, has_side_effects=True, vmem_limit_bytes=60 * 1024 * 1024
        ),
        name="triple_product",
    )(a_tiles, acol, p_tiles, pcol, acol, alen, pcol)
    return out.reshape(1, 7, TILE * TILE)


def solution(mesh):
    in_specs = (
        P("row", "task", None),
        P("row", "task"),
        P("row"),
        P("row", None, None),
        P("row", None),
    )
    out_specs = P(("row", "task"), None, None)
    return jax.shard_map(
        functools.partial(on_device, mesh.shape["row"]),
        mesh=mesh,
        in_specs=in_specs,
        out_specs=out_specs,
        check_vma=False,
    )
```

```python
import functools

import jax
import jax.numpy as jnp
from jax import lax
from jax.experimental import pallas as pl
from jax.experimental.pallas import tpu as pltpu
from jax.sharding import PartitionSpec as P

TILE = 64
RATIO = 8
FW = 6
SLAB = 64
HALF = 32
MESH = pl.DeviceIdType.MESH
F32 = jnp.float32
BF16 = jnp.bfloat16


def split(x):
    high = x.astype(BF16)
    low = (x - high.astype(F32)).astype(BF16)
    return high, low


def kernel(
    row_count,
    a_hbm,
    acol_any,
    p_hbm,
    pcol_any,
    acol,
    alen,
    pcol,
    out_ref,
    a_own,
    a_sib,
    p_raw,
    p_halo,
    acol_sib_v,
    pcol_halo_v,
    acol_sib,
    pcol_halo,
    band_high,
    band_low,
    left,
    ap_high,
    ap_low,
    sums,
    flat,
    sib_out,
    sib_in,
    edge_out,
    edge_in,
    gathered,
    a_local_sem,
    a_send_sem,
    a_recv_sem,
    p_local_sem,
    halo_send_sem,
    halo_recv_sem,
    int_send_sem,
    int_recv_sem,
    int_local_sem,
    cross_send_sem,
    cross_recv_sem,
    sum_send_sem,
    sum_recv_sem,
):
    row = lax.axis_index("row")
    task = lax.axis_index("task")
    core = task % 2
    chip = task // 2
    other = task + 1 - 2 * core
    beside = (row + row_count + 2 * core - 1) % row_count
    has_edge = jnp.logical_or(jnp.logical_and(core == 0, row > 0), jnp.logical_and(core == 1, row < row_count - 1))
    sib_id = (row, other)
    edge_id = (beside, other)

    barrier = pltpu.get_barrier_semaphore()
    for step in range(1, 8):
        pl.semaphore_signal(barrier, inc=1, device_id=(row, (task + step) % 8), device_id_type=MESH)

    @pl.when(has_edge)
    def _():
        pl.semaphore_signal(barrier, inc=1, device_id=edge_id, device_id_type=MESH)

    def home_of(u, which):
        return 3 - u + which * (1 + 2 * u)

    p_copies = []
    for u in (-1, 0, 1, 2, 3):
        first = 32 - 6 * core if u < 0 else 8 * home_of(u, core)
        size = 6 if u < 0 else 8
        copy = pltpu.make_async_copy(
            p_hbm.at[pl.ds(first, size)], p_raw.at[pl.ds(first - 26 * core, size)], p_local_sem.at[u + 1]
        )
        copy.start()
        p_copies.append(copy)
    a_copies = []
    for u in range(4):
        copy = pltpu.make_async_copy(
            a_hbm.at[pl.ds(8 * home_of(u, core), 8)], a_own.at[pl.ds(8 * u, 8)], a_local_sem.at[u]
        )
        copy.start()
        a_copies.append(copy)

    pl.semaphore_wait(barrier, jnp.where(has_edge, 8, 7))

    acol_copy = pltpu.make_async_remote_copy(
        acol_any, acol_sib_v, int_send_sem.at[0], int_recv_sem.at[0], device_id=sib_id, device_id_type=MESH
    )
    acol_copy.start()
    pcol_copy = pltpu.make_async_remote_copy(
        pcol_any, pcol_halo_v, int_send_sem.at[1], int_recv_sem.at[1], device_id=edge_id, device_id_type=MESH
    )
    halo_copy = pltpu.make_async_remote_copy(
        p_hbm.at[pl.ds(58 * core, FW)], p_halo, halo_send_sem, halo_recv_sem, device_id=edge_id, device_id_type=MESH
    )

    @pl.when(has_edge)
    def _():
        pcol_copy.start()
        halo_copy.start()

    a_sends = []
    for u in range(4):
        copy = pltpu.make_async_remote_copy(
            a_hbm.at[pl.ds(8 * home_of(u, 1 - core), 8)],
            a_sib.at[pl.ds(8 * u, 8)],
            a_send_sem.at[u],
            a_recv_sem.at[u],
            device_id=sib_id,
            device_id_type=MESH,
        )
        copy.start()
        a_sends.append(copy)

    lane = lax.broadcasted_iota(jnp.int32, (HALF, 128), 1)
    lower = lane < TILE
    upper_bit = lane // TILE
    parity_order = upper_bit * TILE + 2 * (lane % HALF) + (lane % TILE) // HALF

    def put_band(tiles, index, offset0, offset1, u_parity):
        x0 = tiles[0]
        x1 = tiles[1]
        r0 = pltpu.roll(x0, TILE, 1)
        r1 = pltpu.roll(x1, TILE, 1)
        even0, odd0 = jnp.where(lower, x0, r0), jnp.where(lower, r0, x0)
        even1, odd1 = jnp.where(lower, x1, r1), jnp.where(lower, r1, x1)
        place0 = offset0 + 1 - u_parity
        place1 = offset1 + 1 - u_parity
        for pair in range(2):
            here = upper_bit + 2 * pair
            take0 = here == place0
            take1 = here == place1
            for part, y0, y1 in ((0, even0, even1), (1, odd0, odd1)):
                high, low = split(jnp.where(take0, y0, jnp.where(take1, y1, 0.0)))
                band_high[index, pl.ds(HALF * part, HALF), pl.ds(128 * pair, 128)] = high
                band_low[index, pl.ds(HALF * part, HALF), pl.ds(128 * pair, 128)] = low

    def offset_of(column, home):
        offset = column - home + 1
        return 2 - offset + core * (2 * offset - 2)

    def prepare(u):
        count = 8 if 0 <= u < 4 else FW
        parity = u % 2

        def one(k, carry):
            if u == 4:
                v = 37 - k + core * (2 * k - 5)
                home = 8 * row - 1 + 9 * core
                at = k + 58 * (1 - core)
                tiles = [p_halo[k, pl.ds(which, HALF, stride=2), :] for which in range(2)]
                offsets = [offset_of(pcol_halo[which, at], home) for which in range(2)]
            else:
                j = (32 - 6 * core if u < 0 else 8 * home_of(u, core)) + k
                v = 31 - j + core * (2 * j - 63)
                home = 8 * row + (4 - core if u < 0 else home_of(u, core))
                tiles = [p_raw[j - 26 * core, pl.ds(which, HALF, stride=2), :] for which in range(2)]
                offsets = [offset_of(pcol[which, j], home) for which in range(2)]
            put_band(tiles, v + FW, offsets[0], offsets[1], parity)
            if 0 <= u < 4:
                for d in range(3):
                    zero = jnp.zeros_like(lane)
                    picked = jnp.where(
                        zero + offsets[0] == d, tiles[0], jnp.where(zero + offsets[1] == d, tiles[1], 0.0)
                    )
                    left[u, d, k // 4, pl.ds(HALF * (k % 4), HALF), :] = picked
            return carry

        lax.fori_loop(0, count, one, 0, unroll=2)

    def products(u):
        home = home_of(u, core)

        def one(k, carry):
            j = 8 * home + k
            length = alen[j]
            zero = jnp.zeros((TILE, 128), jnp.int32)
            total = [0.0, 0.0, 0.0]
            for tiles, columns, slot in ((a_own, acol, task), (a_sib, acol_sib, other)):
                column = columns[0, j] - SLAB * row
                v = jnp.clip(31 - column + core * (2 * column - 63), -FW, HALF + FW - 1)
                live = jnp.where(slot < length, 1.0, 0.0).astype(F32)
                raw = tiles[8 * u + k] * live
                near = jnp.take_along_axis(raw, parity_order, axis=1)
                far = pltpu.roll(near, TILE, 1)
                twice = jnp.concatenate([jnp.where(lower, near, far), jnp.where(lower, far, near)], axis=0)
                high, low = split(twice)
                tile = jnp.concatenate([high, low[:, :TILE]], axis=1)
                right_high = band_high[v + FW]
                right_low = band_low[v + FW]
                right = jnp.concatenate([right_high, right_low, right_high], axis=0)
                product = jnp.dot(tile, right, preferred_element_type=F32)
                first, second = product[:, :128], product[:, 128:]
                shift = ((v + 8) // 8 - 2 + 4) // 2 - (u - 2 + 4) // 2
                still = zero + shift == 0
                total[0] = total[0] + jnp.where(still, first, 0.0)
                total[1] = total[1] + jnp.where(still, second, first)
                total[2] = total[2] + jnp.where(still, 0.0, second)
            at = 256 * (k // 4) + HALF * (k % 4)
            for pair in range(3):
                high, low = split(total[pair])
                for part in range(2):
                    place = pl.ds(pl.multiple_of(at + 128 * part, HALF), HALF)
                    lanes = pl.ds(128 * pair, 128)
                    ap_high[place, lanes] = high[HALF * part : HALF * (part + 1)]
                    ap_low[place, lanes] = low[HALF * part : HALF * (part + 1)]
            return carry

        lax.fori_loop(0, 8, one, 0, unroll=2)

    def coarse(u):
        high_parts, low_parts = [], []
        for d in range(3):
            high_row, low_row = [], []
            for group in range(2):
                high, low = split(left[u, d, group].T)
                high_row += [high[:TILE], high[TILE:]]
                low_row += [low[:TILE], low[TILE:]]
            high_parts.append(jnp.concatenate(high_row, axis=1))
            low_parts.append(jnp.concatenate(low_row, axis=1))
        high = jnp.concatenate(high_parts, axis=0)
        low = jnp.concatenate(low_parts, axis=0)
        result = jnp.dot(high, ap_high[...], preferred_element_type=F32)
        result = result + jnp.dot(high, ap_low[...], preferred_element_type=F32)
        result = result + jnp.dot(low, ap_high[...], preferred_element_type=F32)
        for d in range(3):
            begin = (1, 1 - u % 2, 0)[d]
            fresh = d == 2 or u == 0
            for pair in range(4):
                inside = begin <= pair < begin + 3
                if inside:
                    value = result[TILE * d : TILE * (d + 1), 128 * (pair - begin) : 128 * (pair - begin + 1)]
                    if fresh:
                        sums[u + d, pair] = value
                    else:
                        sums[u + d, pair] += value
                elif fresh:
                    sums[u + d, pair] = jnp.zeros((TILE, 128), F32)

    def flatten(w, deltas, target, correction):
        for delta in deltas:
            place = w + delta
            pair = place // 2 - (w - 3) // 2
            even = sums[w + 1, pair, pl.ds(0, HALF, stride=2), :]
            odd = sums[w + 1, pair, pl.ds(1, HALF, stride=2), :]
            if place % 2 == 0:
                value = jnp.where(lower, even, pltpu.roll(odd, TILE, 1))
            else:
                value = jnp.where(lower, pltpu.roll(even, TILE, 1), odd)
            target[3 + (2 * core - 1) * delta - correction] = value

    mine = core == chip // 2

    def sum_copy(w):
        owner = home_of(w, core)
        copy = pltpu.make_async_remote_copy(
            flat.at[w],
            gathered.at[chip],
            sum_send_sem.at[w],
            sum_recv_sem.at[chip],
            device_id=(row, owner),
            device_id_type=MESH,
        )
        return copy, owner == task

    def send_sum(w):
        copy, local = sum_copy(w)

        @pl.when(local)
        def _():
            gathered[chip] = flat[w]

        @pl.when(jnp.logical_not(local))
        def _():
            copy.start()

    sib_copy = pltpu.make_async_remote_copy(
        sib_out, sib_in, cross_send_sem.at[0], cross_recv_sem.at[0], device_id=sib_id, device_id_type=MESH
    )
    edge_copy = pltpu.make_async_remote_copy(
        edge_out, edge_in, cross_send_sem.at[1], cross_recv_sem.at[1], device_id=edge_id, device_id_type=MESH
    )
    everything = range(-3, 4)

    p_copies[0].wait()
    prepare(-1)
    p_copies[1].wait()
    prepare(0)
    p_copies[2].wait()
    prepare(1)
    acol_copy.wait()
    to_smem = pltpu.make_async_copy(acol_sib_v, acol_sib, int_local_sem.at[0])
    to_smem.start()
    to_smem.wait()
    for u in range(4):
        a_copies[u].wait()
        a_sends[u].wait()
        products(u)
        coarse(u)
        if u == 0:
            flatten(-1, range(-1, 4), sib_out, 2 * core)
            sib_copy.start()
            p_copies[3].wait()
            prepare(2)
        elif u == 1:
            flatten(0, everything, flat.at[0], 0)
            sib_copy.wait()
            begin = 2 - 2 * core
            for k in range(5):
                flat[0, begin + k] += sib_in[k]
            send_sum(0)
            p_copies[4].wait()
            prepare(3)
        elif u == 2:
            flatten(1, everything, flat.at[1], 0)
            send_sum(1)

            @pl.when(has_edge)
            def _():
                halo_copy.wait()
                pcol_copy.wait()
                to_smem = pltpu.make_async_copy(pcol_halo_v, pcol_halo, int_local_sem.at[1])
                to_smem.start()
                to_smem.wait()
                prepare(4)

        else:

            @pl.when(has_edge)
            def _():
                flatten(4, range(-3, 2), edge_out, 2 - 2 * core)
                edge_copy.start()

            flatten(2, everything, flat.at[2], 0)
            send_sum(2)
            flatten(3, everything, flat.at[3], 0)

            @pl.when(has_edge)
            def _():
                edge_copy.wait()
                begin = 2 * core
                for k in range(5):
                    flat[3, begin + k] += edge_in[k]

            send_sum(3)

    for w in range(4):
        copy, local = sum_copy(w)

        @pl.when(jnp.logical_not(local))
        def _():
            copy.wait_send()

    for source in range(4):
        copy = pltpu.make_async_remote_copy(
            flat.at[0],
            gathered.at[source],
            sum_send_sem.at[0],
            sum_recv_sem.at[source],
            device_id=(row, other),
            device_id_type=MESH,
        )

        @pl.when(jnp.logical_not(jnp.logical_and(mine, chip == source)))
        def _():
            copy.wait_recv()

    out_ref[...] = (gathered[0] + gathered[1]) + (gathered[2] + gathered[3])


def on_device(row_count, a_vals, a_cols, a_len, p_vals, p_cols):
    a_tiles = a_vals.reshape(SLAB, HALF, 128)
    p_tiles = p_vals.reshape(SLAB, 2, HALF, 128).transpose(0, 2, 1, 3).reshape(SLAB, TILE, 128)
    acol = a_cols.reshape(1, SLAB)
    pcol = p_cols.T
    alen = a_len
    dma = pltpu.SemaphoreType.DMA
    smem = pl.BlockSpec(memory_space=pltpu.SMEM)
    anywhere = pl.BlockSpec(memory_space=pl.ANY)
    out = pl.pallas_call(
        functools.partial(kernel, row_count),
        out_shape=jax.ShapeDtypeStruct((7, HALF, 128), F32),
        in_specs=[anywhere, anywhere, anywhere, anywhere, smem, smem, smem],
        out_specs=pl.BlockSpec(memory_space=pltpu.VMEM),
        scratch_shapes=[
            pltpu.VMEM((HALF, HALF, 128), F32),
            pltpu.VMEM((HALF, HALF, 128), F32),
            pltpu.VMEM((38, TILE, 128), F32),
            pltpu.VMEM((FW, TILE, 128), F32),
            pltpu.VMEM((1, SLAB), jnp.int32),
            pltpu.VMEM((2, SLAB), jnp.int32),
            pltpu.SMEM((1, SLAB), jnp.int32),
            pltpu.SMEM((2, SLAB), jnp.int32),
            pltpu.VMEM((44, TILE, 256), BF16),
            pltpu.VMEM((44, TILE, 256), BF16),
            pltpu.VMEM((4, 3, 2, 128, 128), F32),
            pltpu.VMEM((512, 384), BF16),
            pltpu.VMEM((512, 384), BF16),
            pltpu.VMEM((6, 4, TILE, 128), F32),
            pltpu.VMEM((4, 7, HALF, 128), F32),
            pltpu.VMEM((5, HALF, 128), F32),
            pltpu.VMEM((5, HALF, 128), F32),
            pltpu.VMEM((5, HALF, 128), F32),
            pltpu.VMEM((5, HALF, 128), F32),
            pltpu.VMEM((4, 7, HALF, 128), F32),
            dma((4,)),
            dma((4,)),
            dma((4,)),
            dma((5,)),
            dma,
            dma,
            dma((2,)),
            dma((2,)),
            dma((2,)),
            dma((2,)),
            dma((2,)),
            dma((4,)),
            dma((4,)),
        ],
        compiler_params=pltpu.CompilerParams(
            collective_id=0, has_side_effects=True, vmem_limit_bytes=60 * 1024 * 1024
        ),
        name="triple_product",
    )(a_tiles, acol, p_tiles, pcol, acol, alen, pcol)
    return out.reshape(1, 7, TILE * TILE)


def solution(mesh):
    in_specs = (
        P("row", "task", None),
        P("row", "task"),
        P("row"),
        P("row", None, None),
        P("row", None),
    )
    out_specs = P(("row", "task"), None, None)
    return jax.shard_map(
        functools.partial(on_device, mesh.shape["row"]),
        mesh=mesh,
        in_specs=in_specs,
        out_specs=out_specs,
        check_vma=False,
    )
```

```python
import functools

import jax
import jax.numpy as jnp
from jax import lax
from jax.experimental import pallas as pl
from jax.experimental.pallas import tpu as pltpu
from jax.sharding import PartitionSpec as P

TILE = 64
RATIO = 8
FW = 6
SLAB = 64
HALF = 32
MESH = pl.DeviceIdType.MESH
F32 = jnp.float32
BF16 = jnp.bfloat16


def split(x):
    high = x.astype(BF16)
    low = (x - high.astype(F32)).astype(BF16)
    return high, low


def kernel(
    row_count,
    a_hbm,
    acol_any,
    p_hbm,
    pcol_any,
    alen_any,
    out_ref,
    a_own,
    a_sib,
    p_raw,
    p_halo,
    acol_sib_v,
    pcol_halo_v,
    acol_sib,
    pcol_halo,
    band_high,
    band_low,
    left,
    ap_high,
    ap_low,
    sums,
    flat,
    sib_out,
    sib_in,
    edge_out,
    edge_in,
    gathered,
    a_local_sem,
    a_send_sem,
    a_recv_sem,
    p_local_sem,
    halo_send_sem,
    halo_recv_sem,
    int_send_sem,
    int_recv_sem,
    int_local_sem,
    acol,
    alen,
    pcol,
    cross_send_sem,
    cross_recv_sem,
    sum_send_sem,
    sum_recv_sem,
):
    row = lax.axis_index("row")
    task = lax.axis_index("task")
    core = task % 2
    chip = task // 2
    other = task + 1 - 2 * core
    beside = (row + row_count + 2 * core - 1) % row_count
    has_edge = jnp.logical_or(jnp.logical_and(core == 0, row > 0), jnp.logical_and(core == 1, row < row_count - 1))
    sib_id = (row, other)
    edge_id = (beside, other)

    barrier = pltpu.get_barrier_semaphore()
    for step in range(1, 8):
        pl.semaphore_signal(barrier, inc=1, device_id=(row, (task + step) % 8), device_id_type=MESH)

    @pl.when(has_edge)
    def _():
        pl.semaphore_signal(barrier, inc=1, device_id=edge_id, device_id_type=MESH)

    def home_of(u, which):
        return 3 - u + which * (1 + 2 * u)

    int_copies = []
    for k, (source, target) in enumerate(((acol_any, acol), (alen_any, alen), (pcol_any, pcol))):
        copy = pltpu.make_async_copy(source, target, int_local_sem.at[2 + k])
        copy.start()
        int_copies.append(copy)

    p_copies = []
    for u in (-1, 0, 1, 2, 3):
        first = 32 - 6 * core if u < 0 else 8 * home_of(u, core)
        size = 6 if u < 0 else 8
        copy = pltpu.make_async_copy(
            p_hbm.at[pl.ds(first, size)], p_raw.at[pl.ds(first - 26 * core, size)], p_local_sem.at[u + 1]
        )
        copy.start()
        p_copies.append(copy)
    a_copies = []
    for u in range(4):
        copy = pltpu.make_async_copy(
            a_hbm.at[pl.ds(8 * home_of(u, core), 8)], a_own.at[pl.ds(8 * u, 8)], a_local_sem.at[u]
        )
        copy.start()
        a_copies.append(copy)

    pl.semaphore_wait(barrier, jnp.where(has_edge, 8, 7))

    acol_copy = pltpu.make_async_remote_copy(
        acol_any, acol_sib_v, int_send_sem.at[0], int_recv_sem.at[0], device_id=sib_id, device_id_type=MESH
    )
    acol_copy.start()
    pcol_copy = pltpu.make_async_remote_copy(
        pcol_any, pcol_halo_v, int_send_sem.at[1], int_recv_sem.at[1], device_id=edge_id, device_id_type=MESH
    )
    halo_copy = pltpu.make_async_remote_copy(
        p_hbm.at[pl.ds(58 * core, FW)], p_halo, halo_send_sem, halo_recv_sem, device_id=edge_id, device_id_type=MESH
    )

    @pl.when(has_edge)
    def _():
        pcol_copy.start()
        halo_copy.start()

    a_sends = []
    for u in range(4):
        copy = pltpu.make_async_remote_copy(
            a_hbm.at[pl.ds(8 * home_of(u, 1 - core), 8)],
            a_sib.at[pl.ds(8 * u, 8)],
            a_send_sem.at[u],
            a_recv_sem.at[u],
            device_id=sib_id,
            device_id_type=MESH,
        )
        copy.start()
        a_sends.append(copy)

    sums[...] = jnp.zeros_like(sums)
    lane = lax.broadcasted_iota(jnp.int32, (HALF, 128), 1)
    lower = lane < TILE
    upper_bit = lane // TILE
    parity_order = upper_bit * TILE + 2 * (lane % HALF) + (lane % TILE) // HALF

    def put_band(tiles, index, offset0, offset1, u_parity):
        x0 = tiles[0]
        x1 = tiles[1]
        r0 = pltpu.roll(x0, TILE, 1)
        r1 = pltpu.roll(x1, TILE, 1)
        even0, odd0 = jnp.where(lower, x0, r0), jnp.where(lower, r0, x0)
        even1, odd1 = jnp.where(lower, x1, r1), jnp.where(lower, r1, x1)
        place0 = offset0 + 1 - u_parity
        place1 = offset1 + 1 - u_parity
        for pair in range(2):
            here = upper_bit + 2 * pair
            take0 = here == place0
            take1 = here == place1
            for part, y0, y1 in ((0, even0, even1), (1, odd0, odd1)):
                high, low = split(jnp.where(take0, y0, jnp.where(take1, y1, 0.0)))
                band_high[index, pl.ds(HALF * part, HALF), pl.ds(128 * pair, 128)] = high
                band_low[index, pl.ds(HALF * part, HALF), pl.ds(128 * pair, 128)] = low

    def offset_of(column, home):
        offset = column - home + 1
        return 2 - offset + core * (2 * offset - 2)

    def prepare(u):
        count = 8 if 0 <= u < 4 else FW
        parity = u % 2

        def one(k, carry):
            if u == 4:
                v = 37 - k + core * (2 * k - 5)
                home = 8 * row - 1 + 9 * core
                at = k + 58 * (1 - core)
                tiles = [p_halo[k, pl.ds(which, HALF, stride=2), :] for which in range(2)]
                offsets = [offset_of(pcol_halo[which, at], home) for which in range(2)]
            else:
                j = (32 - 6 * core if u < 0 else 8 * home_of(u, core)) + k
                v = 31 - j + core * (2 * j - 63)
                home = 8 * row + (4 - core if u < 0 else home_of(u, core))
                tiles = [p_raw[j - 26 * core, pl.ds(which, HALF, stride=2), :] for which in range(2)]
                offsets = [offset_of(pcol[which, j], home) for which in range(2)]
            put_band(tiles, v + FW, offsets[0], offsets[1], parity)
            if 0 <= u < 4:
                for d in range(3):
                    zero = jnp.zeros_like(lane)
                    picked = jnp.where(
                        zero + offsets[0] == d, tiles[0], jnp.where(zero + offsets[1] == d, tiles[1], 0.0)
                    )
                    left[u, d, k // 4, pl.ds(HALF * (k % 4), HALF), :] = picked
            return carry

        lax.fori_loop(0, count, one, 0, unroll=True)

    def products(u):
        home = home_of(u, core)

        def one(k, carry):
            j = 8 * home + k
            length = alen[j]
            zero = jnp.zeros((TILE, 128), jnp.int32)
            total = [0.0, 0.0, 0.0]
            for tiles, columns, slot in ((a_own, acol, task), (a_sib, acol_sib, other)):
                column = columns[0, j] - SLAB * row
                v = jnp.clip(31 - column + core * (2 * column - 63), -FW, HALF + FW - 1)
                live = jnp.where(slot < length, 1.0, 0.0).astype(F32)
                raw = tiles[8 * u + k] * live
                near = jnp.take_along_axis(raw, parity_order, axis=1)
                far = pltpu.roll(near, TILE, 1)
                twice = jnp.concatenate([jnp.where(lower, near, far), jnp.where(lower, far, near)], axis=0)
                high, low = split(twice)
                tile = jnp.concatenate([high, low[:, :TILE]], axis=1)
                right_high = band_high[v + FW]
                right_low = band_low[v + FW]
                right = jnp.concatenate([right_high, right_low, right_high], axis=0)
                product = jnp.dot(tile, right, preferred_element_type=F32)
                first, second = product[:, :128], product[:, 128:]
                shift = ((v + 8) // 8 - 2 + 4) // 2 - (u - 2 + 4) // 2
                still = zero + shift == 0
                total[0] = total[0] + jnp.where(still, first, 0.0)
                total[1] = total[1] + jnp.where(still, second, first)
                total[2] = total[2] + jnp.where(still, 0.0, second)
            at = 256 * (k // 4) + HALF * (k % 4)
            for pair in range(3):
                high, low = split(total[pair])
                for part in range(2):
                    place = pl.ds(pl.multiple_of(at + 128 * part, HALF), HALF)
                    lanes = pl.ds(128 * pair, 128)
                    ap_high[place, lanes] = high[HALF * part : HALF * (part + 1)]
                    ap_low[place, lanes] = low[HALF * part : HALF * (part + 1)]
            return carry

        lax.fori_loop(0, 8, one, 0, unroll=True)

    def coarse(u):
        high_parts, low_parts = [], []
        for d in range(3):
            high_row, low_row = [], []
            for group in range(2):
                high, low = split(left[u, d, group].T)
                high_row += [high[:TILE], high[TILE:]]
                low_row += [low[:TILE], low[TILE:]]
            high_parts.append(jnp.concatenate(high_row, axis=1))
            low_parts.append(jnp.concatenate(low_row, axis=1))
        high = jnp.concatenate(high_parts, axis=0)
        low = jnp.concatenate(low_parts, axis=0)
        result = jnp.dot(high, ap_high[...], preferred_element_type=F32)
        result = result + jnp.dot(high, ap_low[...], preferred_element_type=F32)
        result = result + jnp.dot(low, ap_high[...], preferred_element_type=F32)
        for d in range(3):
            begin = (1, 1 - u % 2, 0)[d]
            for pair in range(3):
                sums[u + d, pair + begin] += result[TILE * d : TILE * (d + 1), 128 * pair : 128 * (pair + 1)]

    def flatten(w, deltas, target, correction):
        for delta in deltas:
            place = w + delta
            pair = place // 2 - (w - 3) // 2
            even = sums[w + 1, pair, pl.ds(0, HALF, stride=2), :]
            odd = sums[w + 1, pair, pl.ds(1, HALF, stride=2), :]
            if place % 2 == 0:
                value = jnp.where(lower, even, pltpu.roll(odd, TILE, 1))
            else:
                value = jnp.where(lower, pltpu.roll(even, TILE, 1), odd)
            target[3 + (2 * core - 1) * delta - correction] = value

    mine = core == chip // 2

    def sum_copy(w):
        owner = home_of(w, core)
        copy = pltpu.make_async_remote_copy(
            flat.at[w],
            gathered.at[chip],
            sum_send_sem.at[w],
            sum_recv_sem.at[chip],
            device_id=(row, owner),
            device_id_type=MESH,
        )
        return copy, owner == task

    def send_sum(w):
        copy, local = sum_copy(w)

        @pl.when(local)
        def _():
            gathered[chip] = flat[w]

        @pl.when(jnp.logical_not(local))
        def _():
            copy.start()

    sib_copy = pltpu.make_async_remote_copy(
        sib_out, sib_in, cross_send_sem.at[0], cross_recv_sem.at[0], device_id=sib_id, device_id_type=MESH
    )
    edge_copy = pltpu.make_async_remote_copy(
        edge_out, edge_in, cross_send_sem.at[1], cross_recv_sem.at[1], device_id=edge_id, device_id_type=MESH
    )
    everything = range(-3, 4)

    def work(u):
        a_copies[u].wait()
        a_sends[u].wait()
        products(u)
        coarse(u)

    for copy in int_copies:
        copy.wait()
    p_copies[0].wait()
    prepare(-1)
    for u in range(4):
        p_copies[u + 1].wait()
        prepare(u)
    acol_copy.wait()
    to_smem = pltpu.make_async_copy(acol_sib_v, acol_sib, int_local_sem.at[0])
    to_smem.start()
    to_smem.wait()

    def edge_home():
        @pl.when(has_edge)
        def _():
            pcol_copy.wait()
            to_smem = pltpu.make_async_copy(pcol_halo_v, pcol_halo, int_local_sem.at[1])
            to_smem.start()
            to_smem.wait()
            halo_copy.wait()
            prepare(4)

        work(3)

        @pl.when(has_edge)
        def _():
            flatten(4, range(-3, 2), edge_out, 2 - 2 * core)
            edge_copy.start()

    work(0)
    flatten(-1, range(-1, 4), sib_out, 2 * core)
    sib_copy.start()

    @pl.when(core == 1)
    def _():
        edge_home()

    work(1)
    flatten(0, everything, flat.at[0], 0)
    sib_copy.wait()
    begin = 2 - 2 * core
    for k in range(5):
        flat[0, begin + k] += sib_in[k]
    send_sum(0)

    work(2)
    flatten(1, everything, flat.at[1], 0)
    send_sum(1)

    @pl.when(core == 0)
    def _():
        edge_home()

    flatten(2, everything, flat.at[2], 0)
    send_sum(2)
    flatten(3, everything, flat.at[3], 0)

    @pl.when(has_edge)
    def _():
        edge_copy.wait()
        begin = 2 * core
        for k in range(5):
            flat[3, begin + k] += edge_in[k]

    send_sum(3)

    for w in range(4):
        copy, local = sum_copy(w)

        @pl.when(jnp.logical_not(local))
        def _():
            copy.wait_send()

    for source in range(4):
        copy = pltpu.make_async_remote_copy(
            flat.at[0],
            gathered.at[source],
            sum_send_sem.at[0],
            sum_recv_sem.at[source],
            device_id=(row, other),
            device_id_type=MESH,
        )

        @pl.when(jnp.logical_not(jnp.logical_and(mine, chip == source)))
        def _():
            copy.wait_recv()

    out_ref[...] = (gathered[0] + gathered[1]) + (gathered[2] + gathered[3])


def on_device(row_count, a_vals, a_cols, a_len, p_vals, p_cols):
    a_tiles = a_vals.reshape(SLAB, HALF, 128)
    p_tiles = p_vals.reshape(SLAB, 2, HALF, 128).transpose(0, 2, 1, 3).reshape(SLAB, TILE, 128)
    acol = a_cols.reshape(1, SLAB)
    pcol = p_cols.T
    alen = a_len
    dma = pltpu.SemaphoreType.DMA
    anywhere = pl.BlockSpec(memory_space=pl.ANY)
    out = pl.pallas_call(
        functools.partial(kernel, row_count),
        out_shape=jax.ShapeDtypeStruct((7, HALF, 128), F32),
        in_specs=[anywhere, anywhere, anywhere, anywhere, anywhere],
        out_specs=pl.BlockSpec(memory_space=pltpu.VMEM),
        scratch_shapes=[
            pltpu.VMEM((HALF, HALF, 128), F32),
            pltpu.VMEM((HALF, HALF, 128), F32),
            pltpu.VMEM((38, TILE, 128), F32),
            pltpu.VMEM((FW, TILE, 128), F32),
            pltpu.VMEM((1, SLAB), jnp.int32),
            pltpu.VMEM((2, SLAB), jnp.int32),
            pltpu.SMEM((1, SLAB), jnp.int32),
            pltpu.SMEM((2, SLAB), jnp.int32),
            pltpu.VMEM((44, TILE, 256), BF16),
            pltpu.VMEM((44, TILE, 256), BF16),
            pltpu.VMEM((4, 3, 2, 128, 128), F32),
            pltpu.VMEM((512, 384), BF16),
            pltpu.VMEM((512, 384), BF16),
            pltpu.VMEM((6, 4, TILE, 128), F32),
            pltpu.VMEM((4, 7, HALF, 128), F32),
            pltpu.VMEM((5, HALF, 128), F32),
            pltpu.VMEM((5, HALF, 128), F32),
            pltpu.VMEM((5, HALF, 128), F32),
            pltpu.VMEM((5, HALF, 128), F32),
            pltpu.VMEM((4, 7, HALF, 128), F32),
            dma((4,)),
            dma((4,)),
            dma((4,)),
            dma((5,)),
            dma,
            dma,
            dma((2,)),
            dma((2,)),
            dma((5,)),
            pltpu.SMEM((1, SLAB), jnp.int32),
            pltpu.SMEM((SLAB,), jnp.int32),
            pltpu.SMEM((2, SLAB), jnp.int32),
            dma((2,)),
            dma((2,)),
            dma((4,)),
            dma((4,)),
        ],
        compiler_params=pltpu.CompilerParams(
            collective_id=0, has_side_effects=True, vmem_limit_bytes=60 * 1024 * 1024
        ),
        name="triple_product",
    )(a_tiles, acol, p_tiles, pcol, alen)
    return out.reshape(1, 7, TILE * TILE)


def solution(mesh):
    in_specs = (
        P("row", "task", None),
        P("row", "task"),
        P("row"),
        P("row", None, None),
        P("row", None),
    )
    out_specs = P(("row", "task"), None, None)
    return jax.shard_map(
        functools.partial(on_device, mesh.shape["row"]),
        mesh=mesh,
        in_specs=in_specs,
        out_specs=out_specs,
        check_vma=False,
    )
```

```python
import functools

import jax
import jax.numpy as jnp
from jax import lax
from jax.experimental import pallas as pl
from jax.experimental.pallas import tpu as pltpu
from jax.sharding import PartitionSpec as P

TILE = 64
RATIO = 8
FW = 6
SLAB = 64
HALF = 32
MESH = pl.DeviceIdType.MESH
F32 = jnp.float32
BF16 = jnp.bfloat16


def split(x):
    high = x.astype(BF16)
    low = (x - high.astype(F32)).astype(BF16)
    return high, low


def kernel(
    row_count,
    a_hbm,
    acol_any,
    p_hbm,
    pcol_any,
    alen_any,
    out_ref,
    a_own,
    a_sib,
    p_raw,
    p_halo,
    acol_sib_v,
    pcol_halo_v,
    acol_sib,
    pcol_halo,
    band_high,
    band_low,
    left,
    ap_high,
    ap_low,
    sums,
    flat,
    sib_out,
    sib_in,
    edge_out,
    edge_in,
    gathered,
    a_local_sem,
    a_send_sem,
    a_recv_sem,
    p_local_sem,
    halo_send_sem,
    halo_recv_sem,
    int_send_sem,
    int_recv_sem,
    int_local_sem,
    acol,
    alen,
    pcol,
    cross_send_sem,
    cross_recv_sem,
    sum_send_sem,
    sum_recv_sem,
    last_send_sem,
):
    row = lax.axis_index("row")
    task = lax.axis_index("task")
    core = task % 2
    chip = task // 2
    other = task + 1 - 2 * core
    beside = (row + row_count + 2 * core - 1) % row_count
    has_edge = jnp.logical_or(jnp.logical_and(core == 0, row > 0), jnp.logical_and(core == 1, row < row_count - 1))
    sib_id = (row, other)
    edge_id = (beside, other)

    barrier = pltpu.get_barrier_semaphore()
    for step in range(1, 8):
        pl.semaphore_signal(barrier, inc=1, device_id=(row, (task + step) % 8), device_id_type=MESH)

    @pl.when(has_edge)
    def _():
        pl.semaphore_signal(barrier, inc=1, device_id=edge_id, device_id_type=MESH)

    def home_of(u, which):
        return 3 - u + which * (1 + 2 * u)

    int_copies = []
    for k, (source, target) in enumerate(((acol_any, acol), (alen_any, alen), (pcol_any, pcol))):
        copy = pltpu.make_async_copy(source, target, int_local_sem.at[2 + k])
        copy.start()
        int_copies.append(copy)

    p_copies = []
    for u in (-1, 0, 1, 2, 3):
        first = 32 - 6 * core if u < 0 else 8 * home_of(u, core)
        size = 6 if u < 0 else 8
        copy = pltpu.make_async_copy(
            p_hbm.at[pl.ds(first, size)], p_raw.at[pl.ds(first - 26 * core, size)], p_local_sem.at[u + 1]
        )
        copy.start()
        p_copies.append(copy)
    a_copies = []
    for u in range(4):
        copy = pltpu.make_async_copy(
            a_hbm.at[pl.ds(8 * home_of(u, core), 8)], a_own.at[pl.ds(8 * u, 8)], a_local_sem.at[u]
        )
        copy.start()
        a_copies.append(copy)

    pl.semaphore_wait(barrier, jnp.where(has_edge, 8, 7))

    halo_copy = pltpu.make_async_remote_copy(
        p_hbm.at[pl.ds(58 * core, FW)], p_halo, halo_send_sem, halo_recv_sem, device_id=edge_id, device_id_type=MESH
    )
    pcol_copy = pltpu.make_async_remote_copy(
        pcol_any, pcol_halo_v, int_send_sem.at[1], int_recv_sem.at[1], device_id=edge_id, device_id_type=MESH
    )

    @pl.when(has_edge)
    def _():
        halo_copy.start()
        pcol_copy.start()

    acol_copy = pltpu.make_async_remote_copy(
        acol_any, acol_sib_v, int_send_sem.at[0], int_recv_sem.at[0], device_id=sib_id, device_id_type=MESH
    )
    acol_copy.start()
    a_sends = []
    for u in range(4):
        copy = pltpu.make_async_remote_copy(
            a_hbm.at[pl.ds(8 * home_of(u, 1 - core), 8)],
            a_sib.at[pl.ds(8 * u, 8)],
            a_send_sem.at[u],
            a_recv_sem.at[u],
            device_id=sib_id,
            device_id_type=MESH,
        )
        copy.start()
        a_sends.append(copy)

    sums[...] = jnp.zeros_like(sums)
    lane = lax.broadcasted_iota(jnp.int32, (HALF, 128), 1)
    lower = lane < TILE
    upper_bit = lane // TILE
    parity_order = upper_bit * TILE + 2 * (lane % HALF) + (lane % TILE) // HALF

    def put_band(tiles, index, offset0, offset1, u_parity):
        x0 = tiles[0]
        x1 = tiles[1]
        r0 = pltpu.roll(x0, TILE, 1)
        r1 = pltpu.roll(x1, TILE, 1)
        even0, odd0 = jnp.where(lower, x0, r0), jnp.where(lower, r0, x0)
        even1, odd1 = jnp.where(lower, x1, r1), jnp.where(lower, r1, x1)
        place0 = offset0 + 1 - u_parity
        place1 = offset1 + 1 - u_parity
        for pair in range(2):
            here = upper_bit + 2 * pair
            take0 = here == place0
            take1 = here == place1
            for part, y0, y1 in ((0, even0, even1), (1, odd0, odd1)):
                high, low = split(jnp.where(take0, y0, jnp.where(take1, y1, 0.0)))
                band_high[index, pl.ds(HALF * part, HALF), pl.ds(128 * pair, 128)] = high
                band_low[index, pl.ds(HALF * part, HALF), pl.ds(128 * pair, 128)] = low

    def offset_of(column, home):
        offset = column - home + 1
        return 2 - offset + core * (2 * offset - 2)

    def prepare(u):
        count = 8 if 0 <= u < 4 else FW
        parity = u % 2

        def one(k, carry):
            if u == 4:
                v = 37 - k + core * (2 * k - 5)
                home = 8 * row - 1 + 9 * core
                at = k + 58 * (1 - core)
                tiles = [p_halo[k, pl.ds(which, HALF, stride=2), :] for which in range(2)]
                offsets = [offset_of(pcol_halo[which, at], home) for which in range(2)]
            else:
                j = (32 - 6 * core if u < 0 else 8 * home_of(u, core)) + k
                v = 31 - j + core * (2 * j - 63)
                home = 8 * row + (4 - core if u < 0 else home_of(u, core))
                tiles = [p_raw[j - 26 * core, pl.ds(which, HALF, stride=2), :] for which in range(2)]
                offsets = [offset_of(pcol[which, j], home) for which in range(2)]
            put_band(tiles, v + FW, offsets[0], offsets[1], parity)
            if 0 <= u < 4:
                for d in range(3):
                    zero = jnp.zeros_like(lane)
                    picked = jnp.where(
                        zero + offsets[0] == d, tiles[0], jnp.where(zero + offsets[1] == d, tiles[1], 0.0)
                    )
                    left[u, d, k // 4, pl.ds(HALF * (k % 4), HALF), :] = picked
            return carry

        lax.fori_loop(0, count, one, 0, unroll=True)

    def products(u):
        home = home_of(u, core)

        def one(k, carry):
            j = 8 * home + k
            length = alen[j]
            zero = jnp.zeros((TILE, 128), jnp.int32)
            total = [0.0, 0.0, 0.0]
            for tiles, columns, slot in ((a_own, acol, task), (a_sib, acol_sib, other)):
                column = columns[0, j] - SLAB * row
                v = jnp.clip(31 - column + core * (2 * column - 63), -FW, HALF + FW - 1)
                live = jnp.where(slot < length, 1.0, 0.0).astype(F32)
                raw = tiles[8 * u + k] * live
                near = jnp.take_along_axis(raw, parity_order, axis=1)
                far = pltpu.roll(near, TILE, 1)
                twice = jnp.concatenate([jnp.where(lower, near, far), jnp.where(lower, far, near)], axis=0)
                high, low = split(twice)
                tile = jnp.concatenate([high, low[:, :TILE]], axis=1)
                right_high = band_high[v + FW]
                right_low = band_low[v + FW]
                right = jnp.concatenate([right_high, right_low, right_high], axis=0)
                product = jnp.dot(tile, right, preferred_element_type=F32)
                first, second = product[:, :128], product[:, 128:]
                shift = ((v + 8) // 8 - 2 + 4) // 2 - (u - 2 + 4) // 2
                still = zero + shift == 0
                total[0] = total[0] + jnp.where(still, first, 0.0)
                total[1] = total[1] + jnp.where(still, second, first)
                total[2] = total[2] + jnp.where(still, 0.0, second)
            at = 256 * (k // 4) + HALF * (k % 4)
            for pair in range(3):
                high, low = split(total[pair])
                for part in range(2):
                    place = pl.ds(pl.multiple_of(at + 128 * part, HALF), HALF)
                    lanes = pl.ds(128 * pair, 128)
                    ap_high[place, lanes] = high[HALF * part : HALF * (part + 1)]
                    ap_low[place, lanes] = low[HALF * part : HALF * (part + 1)]
            return carry

        lax.fori_loop(0, 8, one, 0, unroll=True)

    def coarse(u):
        high_parts, low_parts = [], []
        for d in range(3):
            high_row, low_row = [], []
            for group in range(2):
                high, low = split(left[u, d, group].T)
                high_row += [high[:TILE], high[TILE:]]
                low_row += [low[:TILE], low[TILE:]]
            high_parts.append(jnp.concatenate(high_row, axis=1))
            low_parts.append(jnp.concatenate(low_row, axis=1))
        high = jnp.concatenate(high_parts, axis=0)
        low = jnp.concatenate(low_parts, axis=0)
        result = jnp.dot(high, ap_high[...], preferred_element_type=F32)
        result = result + jnp.dot(high, ap_low[...], preferred_element_type=F32)
        result = result + jnp.dot(low, ap_high[...], preferred_element_type=F32)
        for d in range(3):
            begin = (1, 1 - u % 2, 0)[d]
            for pair in range(3):
                sums[u + d, pair + begin] += result[TILE * d : TILE * (d + 1), 128 * pair : 128 * (pair + 1)]

    def flatten(w, deltas, target, correction):
        for delta in deltas:
            place = w + delta
            pair = place // 2 - (w - 3) // 2
            even = sums[w + 1, pair, pl.ds(0, HALF, stride=2), :]
            odd = sums[w + 1, pair, pl.ds(1, HALF, stride=2), :]
            if place % 2 == 0:
                value = jnp.where(lower, even, pltpu.roll(odd, TILE, 1))
            else:
                value = jnp.where(lower, pltpu.roll(even, TILE, 1), odd)
            target[3 + (2 * core - 1) * delta - correction] = value

    mine = core == chip // 2

    def sum_copy(w):
        owner = home_of(w, core)
        copy = pltpu.make_async_remote_copy(
            flat.at[w],
            gathered.at[chip],
            sum_send_sem.at[w],
            sum_recv_sem.at[chip, 0],
            device_id=(row, owner),
            device_id_type=MESH,
        )
        return copy, owner == task

    def send_sum(w):
        copy, local = sum_copy(w)

        @pl.when(local)
        def _():
            gathered[chip] = flat[w]

        @pl.when(jnp.logical_not(local))
        def _():
            copy.start()

    sib_copy = pltpu.make_async_remote_copy(
        sib_out, sib_in, cross_send_sem.at[0], cross_recv_sem.at[0], device_id=sib_id, device_id_type=MESH
    )
    edge_copies = [
        pltpu.make_async_remote_copy(
            edge_out.at[k],
            edge_in.at[k],
            cross_send_sem.at[1 + k],
            cross_recv_sem.at[1 + k],
            device_id=edge_id,
            device_id_type=MESH,
        )
        for k in range(5)
    ]

    last_owner = home_of(3, core)
    last_local = last_owner == task

    def last_copy(k, source):
        place = pl.ds(5 - 5 * core, 2) if k == 5 else pl.ds(2 * core + k, 1)
        return pltpu.make_async_remote_copy(
            flat.at[3, place],
            gathered.at[source, place],
            last_send_sem.at[k],
            sum_recv_sem.at[source, k],
            device_id=(row, last_owner),
            device_id_type=MESH,
        )

    def send_last(k):
        @pl.when(jnp.logical_not(last_local))
        def _():
            last_copy(k, chip).start()

    everything = range(-3, 4)

    def work(u):
        a_copies[u].wait()
        a_sends[u].wait()
        products(u)
        coarse(u)

    for copy in int_copies:
        copy.wait()
    p_copies[0].wait()
    prepare(-1)
    for u in range(4):
        p_copies[u + 1].wait()
        prepare(u)
    acol_copy.wait()
    to_smem = pltpu.make_async_copy(acol_sib_v, acol_sib, int_local_sem.at[0])
    to_smem.start()
    to_smem.wait()

    def edge_home():
        @pl.when(has_edge)
        def _():
            pcol_copy.wait()
            to_smem = pltpu.make_async_copy(pcol_halo_v, pcol_halo, int_local_sem.at[1])
            to_smem.start()
            to_smem.wait()
            halo_copy.wait()
            prepare(4)

        work(3)

        @pl.when(has_edge)
        def _():
            flatten(4, range(-3, 2), edge_out, 2 - 2 * core)
            for copy in edge_copies:
                copy.start()

    work(0)
    flatten(-1, range(-1, 4), sib_out, 2 * core)
    sib_copy.start()

    @pl.when(core == 1)
    def _():
        edge_home()

    work(1)
    flatten(0, everything, flat.at[0], 0)
    sib_copy.wait()
    begin = 2 - 2 * core
    for k in range(5):
        flat[0, begin + k] += sib_in[k]
    send_sum(0)

    work(2)
    flatten(1, everything, flat.at[1], 0)
    send_sum(1)

    @pl.when(core == 0)
    def _():
        edge_home()

    flatten(2, everything, flat.at[2], 0)
    send_sum(2)
    flatten(3, everything, flat.at[3], 0)

    send_last(5)
    for k in range(5):

        @pl.when(has_edge)
        def _():
            edge_copies[k].wait()
            flat[3, 2 * core + k] += edge_in[k]

        send_last(k)

    @pl.when(last_local)
    def _():
        gathered[chip] = flat[3]

    for w in range(3):
        copy, local = sum_copy(w)

        @pl.when(jnp.logical_not(local))
        def _():
            copy.wait_send()

    @pl.when(jnp.logical_not(last_local))
    def _():
        for k in range(6):
            last_copy(k, chip).wait_send()

    owns_last = jnp.logical_or(task == 0, task == 7)
    for source in range(4):
        copy = pltpu.make_async_remote_copy(
            flat.at[0],
            gathered.at[source],
            sum_send_sem.at[0],
            sum_recv_sem.at[source, 0],
            device_id=(row, other),
            device_id_type=MESH,
        )

        elsewhere = jnp.logical_not(jnp.logical_and(mine, chip == source))

        @pl.when(jnp.logical_and(elsewhere, jnp.logical_not(owns_last)))
        def _():
            copy.wait_recv()

        @pl.when(jnp.logical_and(elsewhere, owns_last))
        def _():
            for k in range(6):
                last_copy(k, source).wait_recv()

    out_ref[...] = (gathered[0] + gathered[1]) + (gathered[2] + gathered[3])


def on_device(row_count, a_vals, a_cols, a_len, p_vals, p_cols):
    a_tiles = a_vals.reshape(SLAB, HALF, 128)
    p_tiles = p_vals.reshape(SLAB, 2, HALF, 128).transpose(0, 2, 1, 3).reshape(SLAB, TILE, 128)
    acol = a_cols.reshape(1, SLAB)
    pcol = p_cols.T
    alen = a_len
    dma = pltpu.SemaphoreType.DMA
    anywhere = pl.BlockSpec(memory_space=pl.ANY)
    out = pl.pallas_call(
        functools.partial(kernel, row_count),
        out_shape=jax.ShapeDtypeStruct((7, HALF, 128), F32),
        in_specs=[anywhere, anywhere, anywhere, anywhere, anywhere],
        out_specs=pl.BlockSpec(memory_space=pltpu.VMEM),
        scratch_shapes=[
            pltpu.VMEM((HALF, HALF, 128), F32),
            pltpu.VMEM((HALF, HALF, 128), F32),
            pltpu.VMEM((38, TILE, 128), F32),
            pltpu.VMEM((FW, TILE, 128), F32),
            pltpu.VMEM((1, SLAB), jnp.int32),
            pltpu.VMEM((2, SLAB), jnp.int32),
            pltpu.SMEM((1, SLAB), jnp.int32),
            pltpu.SMEM((2, SLAB), jnp.int32),
            pltpu.VMEM((44, TILE, 256), BF16),
            pltpu.VMEM((44, TILE, 256), BF16),
            pltpu.VMEM((4, 3, 2, 128, 128), F32),
            pltpu.VMEM((512, 384), BF16),
            pltpu.VMEM((512, 384), BF16),
            pltpu.VMEM((6, 4, TILE, 128), F32),
            pltpu.VMEM((4, 7, HALF, 128), F32),
            pltpu.VMEM((5, HALF, 128), F32),
            pltpu.VMEM((5, HALF, 128), F32),
            pltpu.VMEM((5, HALF, 128), F32),
            pltpu.VMEM((5, HALF, 128), F32),
            pltpu.VMEM((4, 7, HALF, 128), F32),
            dma((4,)),
            dma((4,)),
            dma((4,)),
            dma((5,)),
            dma,
            dma,
            dma((2,)),
            dma((2,)),
            dma((5,)),
            pltpu.SMEM((1, SLAB), jnp.int32),
            pltpu.SMEM((SLAB,), jnp.int32),
            pltpu.SMEM((2, SLAB), jnp.int32),
            dma((6,)),
            dma((6,)),
            dma((3,)),
            dma((4, 6)),
            dma((6,)),
        ],
        compiler_params=pltpu.CompilerParams(
            collective_id=0, has_side_effects=True, vmem_limit_bytes=40 * 1024 * 1024
        ),
        name="triple_product",
    )(*[pltpu.with_memory_space_constraint(x, pltpu.HBM) for x in (a_tiles, acol, p_tiles, pcol, alen)])
    return out.reshape(1, 7, TILE * TILE)


def solution(mesh):
    in_specs = (
        P("row", "task", None),
        P("row", "task"),
        P("row"),
        P("row", None, None),
        P("row", None),
    )
    out_specs = P(("row", "task"), None, None)
    return jax.shard_map(
        functools.partial(on_device, mesh.shape["row"]),
        mesh=mesh,
        in_specs=in_specs,
        out_specs=out_specs,
        check_vma=False,
    )
```

```python
import functools

import jax
import jax.numpy as jnp
from jax import lax
from jax.experimental import pallas as pl
from jax.experimental.pallas import tpu as pltpu
from jax.sharding import PartitionSpec as P

TILE = 64
RATIO = 8
FW = 6
SLAB = 64
HALF = 32
MESH = pl.DeviceIdType.MESH
F32 = jnp.float32
BF16 = jnp.bfloat16


def split(x):
    high = x.astype(BF16)
    low = (x - high.astype(F32)).astype(BF16)
    return high, low


def kernel(
    row_count,
    a_hbm,
    acol_any,
    p_hbm,
    pcol_any,
    alen_any,
    out_ref,
    a_own,
    a_sib,
    p_raw,
    p_halo,
    acol_sib_v,
    pcol_halo_v,
    acol_sib,
    pcol_halo,
    band_high,
    band_low,
    left,
    stage_tiles,
    stage_rows,
    ap_high,
    ap_low,
    sums,
    flat,
    sib_out,
    sib_in,
    edge_out,
    edge_in,
    gathered,
    a_local_sem,
    a_send_sem,
    a_recv_sem,
    p_local_sem,
    halo_send_sem,
    halo_recv_sem,
    int_send_sem,
    int_recv_sem,
    int_local_sem,
    acol,
    alen,
    pcol,
    cross_send_sem,
    cross_recv_sem,
    sum_send_sem,
    sum_recv_sem,
    last_send_sem,
):
    row = lax.axis_index("row")
    task = lax.axis_index("task")
    core = task % 2
    chip = task // 2
    other = task + 1 - 2 * core
    beside = (row + row_count + 2 * core - 1) % row_count
    has_edge = jnp.logical_or(jnp.logical_and(core == 0, row > 0), jnp.logical_and(core == 1, row < row_count - 1))
    sib_id = (row, other)
    edge_id = (beside, other)

    barrier = pltpu.get_barrier_semaphore()
    for step in range(1, 8):
        pl.semaphore_signal(barrier, inc=1, device_id=(row, (task + step) % 8), device_id_type=MESH)

    @pl.when(has_edge)
    def _():
        pl.semaphore_signal(barrier, inc=1, device_id=edge_id, device_id_type=MESH)

    def home_of(u, which):
        return 3 - u + which * (1 + 2 * u)

    int_copies = []
    for k, (source, target) in enumerate(((acol_any, acol), (alen_any, alen), (pcol_any, pcol))):
        copy = pltpu.make_async_copy(source, target, int_local_sem.at[2 + k])
        copy.start()
        int_copies.append(copy)

    p_copies = []
    for u in (-1, 0, 1, 2, 3):
        first = 32 - 6 * core if u < 0 else 8 * home_of(u, core)
        size = 6 if u < 0 else 8
        copy = pltpu.make_async_copy(
            p_hbm.at[pl.ds(first, size)], p_raw.at[pl.ds(first - 26 * core, size)], p_local_sem.at[u + 1]
        )
        copy.start()
        p_copies.append(copy)
    a_copies = []
    for u in range(4):
        copy = pltpu.make_async_copy(
            a_hbm.at[pl.ds(8 * home_of(u, core), 8)], a_own.at[pl.ds(8 * u, 8)], a_local_sem.at[u]
        )
        copy.start()
        a_copies.append(copy)

    pl.semaphore_wait(barrier, jnp.where(has_edge, 8, 7))

    halo_copy = pltpu.make_async_remote_copy(
        p_hbm.at[pl.ds(58 * core, FW)], p_halo, halo_send_sem, halo_recv_sem, device_id=edge_id, device_id_type=MESH
    )
    pcol_copy = pltpu.make_async_remote_copy(
        pcol_any, pcol_halo_v, int_send_sem.at[1], int_recv_sem.at[1], device_id=edge_id, device_id_type=MESH
    )

    @pl.when(has_edge)
    def _():
        halo_copy.start()
        pcol_copy.start()

    acol_copy = pltpu.make_async_remote_copy(
        acol_any, acol_sib_v, int_send_sem.at[0], int_recv_sem.at[0], device_id=sib_id, device_id_type=MESH
    )
    acol_copy.start()
    a_sends = []
    for u in range(4):
        copy = pltpu.make_async_remote_copy(
            a_hbm.at[pl.ds(8 * home_of(u, 1 - core), 8)],
            a_sib.at[pl.ds(8 * u, 8)],
            a_send_sem.at[u],
            a_recv_sem.at[u],
            device_id=sib_id,
            device_id_type=MESH,
        )
        copy.start()
        a_sends.append(copy)

    sums[...] = jnp.zeros_like(sums)
    lane = lax.broadcasted_iota(jnp.int32, (HALF, 128), 1)
    lower = lane < TILE
    upper_bit = lane // TILE
    parity_order = upper_bit * TILE + 2 * (lane % HALF) + (lane % TILE) // HALF

    def put_band(tiles, index, offset0, offset1, u_parity):
        x0 = tiles[0]
        x1 = tiles[1]
        r0 = pltpu.roll(x0, TILE, 1)
        r1 = pltpu.roll(x1, TILE, 1)
        even0, odd0 = jnp.where(lower, x0, r0), jnp.where(lower, r0, x0)
        even1, odd1 = jnp.where(lower, x1, r1), jnp.where(lower, r1, x1)
        place0 = offset0 + 1 - u_parity
        place1 = offset1 + 1 - u_parity
        for pair in range(2):
            here = upper_bit + 2 * pair
            take0 = here == place0
            take1 = here == place1
            for part, y0, y1 in ((0, even0, even1), (1, odd0, odd1)):
                high, low = split(jnp.where(take0, y0, jnp.where(take1, y1, 0.0)))
                band_high[index, pl.ds(HALF * part, HALF), pl.ds(128 * pair, 128)] = high
                band_low[index, pl.ds(HALF * part, HALF), pl.ds(128 * pair, 128)] = low

    def offset_of(column, home):
        offset = column - home + 1
        return 2 - offset + core * (2 * offset - 2)

    def prepare(u):
        count = 8 if 0 <= u < 4 else FW
        parity = u % 2

        def one(k, carry):
            if u == 4:
                v = 37 - k + core * (2 * k - 5)
                home = 8 * row - 1 + 9 * core
                at = k + 58 * (1 - core)
                tiles = [p_halo[k, pl.ds(which, HALF, stride=2), :] for which in range(2)]
                offsets = [offset_of(pcol_halo[which, at], home) for which in range(2)]
            else:
                j = (32 - 6 * core if u < 0 else 8 * home_of(u, core)) + k
                v = 31 - j + core * (2 * j - 63)
                home = 8 * row + (4 - core if u < 0 else home_of(u, core))
                tiles = [p_raw[j - 26 * core, pl.ds(which, HALF, stride=2), :] for which in range(2)]
                offsets = [offset_of(pcol[which, j], home) for which in range(2)]
            put_band(tiles, v + FW, offsets[0], offsets[1], parity)
            if 0 <= u < 4:
                for d in range(3):
                    zero = jnp.zeros_like(lane)
                    picked = jnp.where(
                        zero + offsets[0] == d, tiles[0], jnp.where(zero + offsets[1] == d, tiles[1], 0.0)
                    )
                    left[u, d, k // 4, pl.ds(HALF * (k % 4), HALF), :] = picked
            return carry

        lax.fori_loop(0, count, one, 0, unroll=True)

    def left_tile(tiles, slot, u, k):
        live = jnp.where(slot < alen[8 * home_of(u, core) + k], 1.0, 0.0).astype(F32)
        raw = tiles[8 * u + k] * live
        near = jnp.take_along_axis(raw, parity_order, axis=1)
        far = pltpu.roll(near, TILE, 1)
        high, low = split(jnp.concatenate([jnp.where(lower, near, far), jnp.where(lower, far, near)], axis=0))
        return jnp.concatenate([high, low[:, :TILE]], axis=1)

    def left_rows(u):
        high_parts, low_parts = [], []
        for d in range(3):
            high_row, low_row = [], []
            for group in range(2):
                high, low = split(left[u, d, group].T)
                high_row += [high[:TILE], high[TILE:]]
                low_row += [low[:TILE], low[TILE:]]
            high_parts.append(jnp.concatenate(high_row, axis=1))
            low_parts.append(jnp.concatenate(low_row, axis=1))
        return jnp.concatenate(high_parts, axis=0), jnp.concatenate(low_parts, axis=0)

    def stage(u):
        def one(k, carry):
            stage_tiles[2 * k] = left_tile(a_own, task, u, k)
            stage_tiles[2 * k + 1] = left_tile(a_sib, other, u, k)
            return carry

        lax.fori_loop(0, 8, one, 0, unroll=True)
        stage_rows[0], stage_rows[1] = left_rows(u)

    def products(u, staged):
        home = home_of(u, core)

        def one(k, carry):
            j = 8 * home + k
            zero = jnp.zeros((TILE, 128), jnp.int32)
            total = [0.0, 0.0, 0.0]
            for which, (tiles, columns, slot) in enumerate(((a_own, acol, task), (a_sib, acol_sib, other))):
                column = columns[0, j] - SLAB * row
                v = jnp.clip(31 - column + core * (2 * column - 63), -FW, HALF + FW - 1)
                tile = stage_tiles[2 * k + which] if staged else left_tile(tiles, slot, u, k)
                right_high = band_high[v + FW]
                right_low = band_low[v + FW]
                right = jnp.concatenate([right_high, right_low, right_high], axis=0)
                product = jnp.dot(tile, right, preferred_element_type=F32)
                first, second = product[:, :128], product[:, 128:]
                shift = ((v + 8) // 8 - 2 + 4) // 2 - (u - 2 + 4) // 2
                still = zero + shift == 0
                total[0] = total[0] + jnp.where(still, first, 0.0)
                total[1] = total[1] + jnp.where(still, second, first)
                total[2] = total[2] + jnp.where(still, 0.0, second)
            at = 256 * (k // 4) + HALF * (k % 4)
            for pair in range(3):
                high, low = split(total[pair])
                for part in range(2):
                    place = pl.ds(pl.multiple_of(at + 128 * part, HALF), HALF)
                    lanes = pl.ds(128 * pair, 128)
                    ap_high[place, lanes] = high[HALF * part : HALF * (part + 1)]
                    ap_low[place, lanes] = low[HALF * part : HALF * (part + 1)]
            return carry

        lax.fori_loop(0, 8, one, 0, unroll=True)

    def coarse(u, staged):
        high, low = (stage_rows[0], stage_rows[1]) if staged else left_rows(u)
        result = jnp.dot(high, ap_high[...], preferred_element_type=F32)
        result = result + jnp.dot(high, ap_low[...], preferred_element_type=F32)
        result = result + jnp.dot(low, ap_high[...], preferred_element_type=F32)
        for d in range(3):
            begin = (1, 1 - u % 2, 0)[d]
            for pair in range(3):
                sums[u + d, pair + begin] += result[TILE * d : TILE * (d + 1), 128 * pair : 128 * (pair + 1)]

    def flatten(w, deltas, target, correction):
        for delta in deltas:
            place = w + delta
            pair = place // 2 - (w - 3) // 2
            even = sums[w + 1, pair, pl.ds(0, HALF, stride=2), :]
            odd = sums[w + 1, pair, pl.ds(1, HALF, stride=2), :]
            if place % 2 == 0:
                value = jnp.where(lower, even, pltpu.roll(odd, TILE, 1))
            else:
                value = jnp.where(lower, pltpu.roll(even, TILE, 1), odd)
            target[3 + (2 * core - 1) * delta - correction] = value

    mine = core == chip // 2

    def sum_copy(w):
        owner = home_of(w, core)
        copy = pltpu.make_async_remote_copy(
            flat.at[w],
            gathered.at[chip],
            sum_send_sem.at[w],
            sum_recv_sem.at[chip, 0],
            device_id=(row, owner),
            device_id_type=MESH,
        )
        return copy, owner == task

    def send_sum(w):
        copy, local = sum_copy(w)

        @pl.when(local)
        def _():
            gathered[chip] = flat[w]

        @pl.when(jnp.logical_not(local))
        def _():
            copy.start()

    sib_copy = pltpu.make_async_remote_copy(
        sib_out, sib_in, cross_send_sem.at[0], cross_recv_sem.at[0], device_id=sib_id, device_id_type=MESH
    )
    edge_copies = [
        pltpu.make_async_remote_copy(
            edge_out.at[k],
            edge_in.at[k],
            cross_send_sem.at[1 + k],
            cross_recv_sem.at[1 + k],
            device_id=edge_id,
            device_id_type=MESH,
        )
        for k in range(5)
    ]

    last_owner = home_of(3, core)
    last_local = last_owner == task

    def last_copy(k, source):
        place = pl.ds(5 - 5 * core, 2) if k == 5 else pl.ds(2 * core + k, 1)
        return pltpu.make_async_remote_copy(
            flat.at[3, place],
            gathered.at[source, place],
            last_send_sem.at[k],
            sum_recv_sem.at[source, k],
            device_id=(row, last_owner),
            device_id_type=MESH,
        )

    next_owner = home_of(2, core)
    next_local = next_owner == task

    def next_copy(k, source):
        place = pl.ds(5 - 5 * core, 2) if k == 1 else pl.ds(2 * core, 5)
        return pltpu.make_async_remote_copy(
            flat.at[2, place],
            gathered.at[source, place],
            sum_send_sem.at[2 + k],
            sum_recv_sem.at[source, k],
            device_id=(row, next_owner),
            device_id_type=MESH,
        )

    def send_next(k):
        @pl.when(jnp.logical_not(next_local))
        def _():
            next_copy(k, chip).start()

    def send_last(k):
        @pl.when(jnp.logical_not(last_local))
        def _():
            last_copy(k, chip).start()

    everything = range(-3, 4)

    def work(u):
        if u < 3:
            a_copies[u].wait()
            a_sends[u].wait()
        products(u, u == 3)
        coarse(u, u == 3)

    for copy in int_copies:
        copy.wait()
    p_copies[0].wait()
    prepare(-1)
    for u in range(4):
        p_copies[u + 1].wait()
        prepare(u)
    acol_copy.wait()
    to_smem = pltpu.make_async_copy(acol_sib_v, acol_sib, int_local_sem.at[0])
    to_smem.start()
    to_smem.wait()

    def edge_home():
        a_copies[3].wait()
        a_sends[3].wait()
        stage(3)

        @pl.when(has_edge)
        def _():
            pcol_copy.wait()
            to_smem = pltpu.make_async_copy(pcol_halo_v, pcol_halo, int_local_sem.at[1])
            to_smem.start()
            to_smem.wait()
            halo_copy.wait()
            prepare(4)

        work(3)

        @pl.when(has_edge)
        def _():
            flatten(4, range(-3, 2), edge_out, 2 - 2 * core)
            for copy in edge_copies:
                copy.start()

    work(0)
    flatten(-1, range(-1, 4), sib_out, 2 * core)
    sib_copy.start()

    @pl.when(core == 1)
    def _():
        edge_home()

    work(1)
    flatten(0, everything, flat.at[0], 0)
    sib_copy.wait()
    begin = 2 - 2 * core
    for k in range(5):
        flat[0, begin + k] += sib_in[k]
    send_sum(0)

    work(2)
    flatten(1, everything, flat.at[1], 0)
    send_sum(1)

    flatten(2, (-3, -2), flat.at[2], 0)
    send_next(1)

    @pl.when(core == 0)
    def _():
        edge_home()

    flatten(2, range(-1, 4), flat.at[2], 0)
    send_next(0)

    @pl.when(next_local)
    def _():
        gathered[chip] = flat[2]

    flatten(3, everything, flat.at[3], 0)

    send_last(5)
    for k in range(5):

        @pl.when(has_edge)
        def _():
            edge_copies[k].wait()
            flat[3, 2 * core + k] += edge_in[k]

        send_last(k)

    @pl.when(last_local)
    def _():
        gathered[chip] = flat[3]

    for w in range(2):
        copy, local = sum_copy(w)

        @pl.when(jnp.logical_not(local))
        def _():
            copy.wait_send()

    @pl.when(jnp.logical_not(last_local))
    def _():
        for k in range(6):
            last_copy(k, chip).wait_send()

    @pl.when(jnp.logical_not(next_local))
    def _():
        for k in range(2):
            next_copy(k, chip).wait_send()

    owns_last = jnp.logical_or(task == 0, task == 7)
    owns_next = jnp.logical_or(task == 1, task == 6)
    for source in range(4):
        copy = pltpu.make_async_remote_copy(
            flat.at[0],
            gathered.at[source],
            sum_send_sem.at[0],
            sum_recv_sem.at[source, 0],
            device_id=(row, other),
            device_id_type=MESH,
        )

        elsewhere = jnp.logical_not(jnp.logical_and(mine, chip == source))

        @pl.when(jnp.logical_and(elsewhere, jnp.logical_not(jnp.logical_or(owns_last, owns_next))))
        def _():
            copy.wait_recv()

        @pl.when(jnp.logical_and(elsewhere, owns_next))
        def _():
            for k in range(2):
                next_copy(k, source).wait_recv()

        @pl.when(jnp.logical_and(elsewhere, owns_last))
        def _():
            for k in range(6):
                last_copy(k, source).wait_recv()

    out_ref[...] = (gathered[0] + gathered[1]) + (gathered[2] + gathered[3])


def on_device(row_count, a_vals, a_cols, a_len, p_vals, p_cols):
    a_tiles = a_vals.reshape(SLAB, HALF, 128)
    p_tiles = p_vals.reshape(SLAB, 2, HALF, 128).transpose(0, 2, 1, 3).reshape(SLAB, TILE, 128)
    acol = a_cols.reshape(1, SLAB)
    pcol = p_cols.T
    alen = a_len
    dma = pltpu.SemaphoreType.DMA
    anywhere = pl.BlockSpec(memory_space=pl.ANY)
    out = pl.pallas_call(
        functools.partial(kernel, row_count),
        out_shape=jax.ShapeDtypeStruct((7, HALF, 128), F32),
        in_specs=[anywhere, anywhere, anywhere, anywhere, anywhere],
        out_specs=pl.BlockSpec(memory_space=pltpu.VMEM),
        scratch_shapes=[
            pltpu.VMEM((HALF, HALF, 128), F32),
            pltpu.VMEM((HALF, HALF, 128), F32),
            pltpu.VMEM((38, TILE, 128), F32),
            pltpu.VMEM((FW, TILE, 128), F32),
            pltpu.VMEM((1, SLAB), jnp.int32),
            pltpu.VMEM((2, SLAB), jnp.int32),
            pltpu.SMEM((1, SLAB), jnp.int32),
            pltpu.SMEM((2, SLAB), jnp.int32),
            pltpu.VMEM((44, TILE, 256), BF16),
            pltpu.VMEM((44, TILE, 256), BF16),
            pltpu.VMEM((4, 3, 2, 128, 128), F32),
            pltpu.VMEM((16, TILE, 192), BF16),
            pltpu.VMEM((2, 192, 512), BF16),
            pltpu.VMEM((512, 384), BF16),
            pltpu.VMEM((512, 384), BF16),
            pltpu.VMEM((6, 4, TILE, 128), F32),
            pltpu.VMEM((4, 7, HALF, 128), F32),
            pltpu.VMEM((5, HALF, 128), F32),
            pltpu.VMEM((5, HALF, 128), F32),
            pltpu.VMEM((5, HALF, 128), F32),
            pltpu.VMEM((5, HALF, 128), F32),
            pltpu.VMEM((4, 7, HALF, 128), F32),
            dma((4,)),
            dma((4,)),
            dma((4,)),
            dma((5,)),
            dma,
            dma,
            dma((2,)),
            dma((2,)),
            dma((5,)),
            pltpu.SMEM((1, SLAB), jnp.int32),
            pltpu.SMEM((SLAB,), jnp.int32),
            pltpu.SMEM((2, SLAB), jnp.int32),
            dma((6,)),
            dma((6,)),
            dma((4,)),
            dma((4, 6)),
            dma((6,)),
        ],
        compiler_params=pltpu.CompilerParams(
            collective_id=0, has_side_effects=True, vmem_limit_bytes=40 * 1024 * 1024
        ),
        name="triple_product",
    )(*[pltpu.with_memory_space_constraint(x, pltpu.HBM) for x in (a_tiles, acol, p_tiles, pcol, alen)])
    return out.reshape(1, 7, TILE * TILE)


def solution(mesh):
    in_specs = (
        P("row", "task", None),
        P("row", "task"),
        P("row"),
        P("row", None, None),
        P("row", None),
    )
    out_specs = P(("row", "task"), None, None)
    return jax.shard_map(
        functools.partial(on_device, mesh.shape["row"]),
        mesh=mesh,
        in_specs=in_specs,
        out_specs=out_specs,
        check_vma=False,
    )
```
